128 devices in a mesh: tm: 8 (over z, x_hi), space: 16 (over x_lo, y, core).
Axes of the slice: x: 4 (x_hi: 2, x_lo: 2; x = x_hi * 2 + x_lo), y: 4, z: 4, core: 2. Of those that a mesh axis runs over, the one named last changes fastest.
Arguments:
- solutions: bfloat16 [128, 64, 2, 3, 8192], P(('tm', 'space')), may hold values from -6 to 6
- eigvecs: bfloat16 [128, 128, 2, 3, 8192], P('tm', None, None, None, 'space'), may hold values from -0.02734375 to 0.02734375
Outputs:
- perambulator: float32 [128, 128, 128], P('tm', 'space')
The draws below stay inside these ranges and needn't reach their ends.
All inputs are finite; a program needn't handle non-finite values.
Results may differ from the reference program's by a relative error of at most 0.0003.
Values may be sent and summed in bfloat16 or wider, within the bound.
No kernel may reach another device: no remote copies, remote signals or barrier semaphores. Data moves between devices by JAX's collectives and lax.ppermute only.
A program may use at most 192 MiB of HBM per device.

```python
import jax
import jax.numpy as jnp
from jax import lax

NEV = 128
COLORS = 3
SC = 64
VOL = 8192
TSL = 128


def block_levels(rng, shape, shards, least, top_value):
    def one(position, parts):
        steps = jax.random.uniform(jax.random.fold_in(jax.random.fold_in(rng, 6), position), (parts,), jnp.float32, least / len(shards), top_value / len(shards))
        return jnp.repeat(jnp.exp(steps), shape[position] // parts).reshape((-1,) + (1,) * (len(shape) - position - 1))

    level = one(*shards[0])
    for cut in shards[1:]:
        level = level * one(*cut)
    return level


def centred(key, shape, width, reach, split=(), dtype=jnp.bfloat16):
    entries = jax.random.normal(key, shape, jnp.float32) * width
    if len(split) > 0:
        entries = block_levels(key, shape, split, -0.22, 0.18) * entries
    return jnp.clip(entries, min=-reach, max=reach).astype(dtype)


def setup_inputs(seed: int = 0) -> dict:
    seeds = jax.random.split(jax.random.key(seed), 3)
    return {
        "solutions": centred(seeds[0], (TSL, SC, 2, COLORS, VOL), 1.0, 6.0, ((0, 128),)),
        "eigvecs": centred(seeds[1], (TSL, NEV, 2, COLORS, VOL), (6 * VOL) ** -0.5, 0.02734375, ((0, 8), (4, 16))),
    }


def project_slice(pair):
    vectors, fields = pair
    vectors = vectors.astype(jnp.float32)
    fields = fields.astype(jnp.float32)
    real_part = jnp.einsum("nrcx,mrcx->nm", vectors, fields, precision=lax.Precision.HIGHEST)
    imag_part = jnp.einsum("ncx,mcx->nm", vectors[:, 0], fields[:, 1], precision=lax.Precision.HIGHEST)
    imag_part = imag_part - jnp.einsum("ncx,mcx->nm", vectors[:, 1], fields[:, 0], precision=lax.Precision.HIGHEST)
    return jnp.concatenate([real_part, imag_part], axis=1)


def reference(solutions, eigvecs):
    return lax.map(project_slice, (eigvecs, solutions))
```

```python
import jax
import jax.numpy as jnp
from jax import lax
from jax.experimental import pallas as pl
from jax.experimental.pallas import tpu as pltpu
from jax.sharding import PartitionSpec as P

LANES = 128


def tile_view(a, groups):
    outer, rows, parts, colors, sites = a.shape
    a = a.reshape(outer, rows, parts, colors, groups, sites // groups // LANES, LANES)
    a = a.transpose(0, 1, 3, 4, 5, 2, 6)
    return a.reshape(outer, rows, colors, groups, -1, LANES)


def unpack_kernel(src, dst, wide):
    _, rows, colors, groups, inner, _ = src.shape
    stride = colors * groups * inner
    wide[...] = src[...].astype(jnp.float32).reshape(wide.shape)
    for g in range(groups):
        for c in range(colors):
            for k in range(inner):
                lines = wide[pl.ds((c * groups + g) * inner + k, rows, stride=stride), :]
                lane = (c * (inner // 2) + k // 2) * LANES
                dst[g, k % 2, :, pl.ds(lane, LANES)] = lines.astype(jnp.bfloat16)


def unpack(view, block_rows):
    outer, rows, colors, groups, inner, _ = view.shape
    depth = colors * inner // 2 * LANES
    return pl.pallas_call(
        unpack_kernel,
        grid=(outer, rows // block_rows),
        in_specs=[
            pl.BlockSpec((1, block_rows, colors, groups, inner, LANES), lambda a, b: (a, b, 0, 0, 0, 0))
        ],
        out_specs=pl.BlockSpec((groups, 2, block_rows, depth), lambda a, b: (a, 0, b, 0)),
        out_shape=jax.ShapeDtypeStruct((outer * groups, 2, rows, depth), view.dtype),
        scratch_shapes=[pltpu.VMEM((block_rows * colors * groups * inner, LANES), jnp.float32)],
        compiler_params=pltpu.CompilerParams(vmem_limit_bytes=40 * 2**20),
        cost_estimate=pl.CostEstimate(flops=0, bytes_accessed=4 * view.size, transcendentals=0),
    )(view)


def product_kernel(vec, sol, out):
    rows = vec.shape[2]
    cols = sol.shape[2]
    e = vec[0].reshape(2 * rows, vec.shape[3])
    s = sol[0].reshape(2 * cols, sol.shape[3])
    g = lax.dot_general(e, s, (((1,), (1,)), ((), ())), preferred_element_type=jnp.float32)
    crossed = pltpu.roll(g[rows:], cols, 1)
    lane = lax.broadcasted_iota(jnp.int32, crossed.shape, 1)
    res = g[:rows] + jnp.where(lane < cols, crossed, -crossed)
    out[...] = res.reshape(out.shape)


def product(vec, sol, shares):
    times, _, rows, depth = vec.shape
    cols = sol.shape[2]
    return pl.pallas_call(
        product_kernel,
        grid=(times,),
        in_specs=[
            pl.BlockSpec((1, 2, rows, depth), lambda t: (t, 0, 0, 0)),
            pl.BlockSpec((1, 2, cols, depth), lambda t: (t, 0, 0, 0)),
        ],
        out_specs=pl.BlockSpec((shares, 1, rows // shares, 2 * cols), lambda t: (0, t, 0, 0)),
        out_shape=jax.ShapeDtypeStruct((shares, times, rows // shares, 2 * cols), jnp.float32),
        compiler_params=pltpu.CompilerParams(vmem_limit_bytes=40 * 2**20),
        cost_estimate=pl.CostEstimate(
            flops=8 * times * rows * cols * depth, bytes_accessed=2 * (vec.size + sol.size), transcendentals=0
        ),
    )(vec, sol)


def body(solutions, eigvecs):
    shares = lax.axis_size("space")
    sol = unpack(tile_view(solutions, shares), 16)
    sol = lax.all_to_all(sol, "space", split_axis=0, concat_axis=0, tiled=True)
    vec = unpack(tile_view(eigvecs, 1), eigvecs.shape[1])
    partial = product(vec, sol, shares)
    partial = lax.all_to_all(partial, "space", split_axis=0, concat_axis=0, tiled=True)
    return jnp.sum(partial, axis=0)


def solution(mesh):
    placed = (P(("tm", "space"), None, None, None, None), P("tm", None, None, None, "space"))
    return jax.shard_map(
        body, mesh=mesh, in_specs=placed, out_specs=P("tm", "space", None), check_vma=False
    )
```

```python
import jax
import jax.numpy as jnp
from jax import lax
from jax.experimental import pallas as pl
from jax.experimental.pallas import tpu as pltpu
from jax.sharding import PartitionSpec as P

LANES = 128
VMEM = 16 * 2**20
PACK_VMEM = 52 * 2**20
FREE = pl.CostEstimate(flops=0, bytes_accessed=0, transcendentals=0)
RING = 4
MOVES = [(1, 0), (0, 2), (1, 1), (1, 3), (0, 3), (0, 1), (1, 2)]


def tile_view(a, groups):
    outer, rows, parts, colors, sites = a.shape
    a = a.reshape(outer, rows, parts, colors, groups, sites // groups // LANES, LANES)
    a = a.transpose(0, 1, 3, 4, 5, 2, 6)
    return a.reshape(outer, rows, colors, groups, -1, LANES)


def split_lines(src, dst, wide, flip):
    _, rows, colors, groups, inner, _ = src.shape
    lines = colors * groups * inner
    stride = wide.shape[0] // rows
    for i in range(rows):
        wide[i * stride : i * stride + lines] = src[0, i].astype(jnp.float32).reshape(lines, LANES)
    for g in range(groups):
        for c in range(colors):
            for k in range(inner):
                picked = wide[pl.ds((c * groups + g) * inner + k, rows, stride=stride), :]
                lane = (c * (inner // 2) + k // 2) * LANES
                dst[g ^ flip, k % 2, :, pl.ds(lane, LANES)] = picked.astype(jnp.bfloat16)


def pack_solutions(view, where, block_rows=32):
    _, rows, colors, groups, inner, _ = view.shape
    count = where.shape[0] - 1
    depth = colors * inner // 2 * LANES

    def kernel(where, *refs):
        for n in range(count):
            split_lines(refs[n], refs[count + n], refs[2 * count], where[count])

    def source(n):
        return pl.BlockSpec(
            (1, block_rows, colors, 2, inner, LANES), lambda b, where: (0, b, 0, where[n], 0, 0)
        )

    return pl.pallas_call(
        kernel,
        grid_spec=pltpu.PrefetchScalarGridSpec(
            num_scalar_prefetch=1,
            grid=(rows // block_rows,),
            in_specs=[source(n) for n in range(count)],
            out_specs=[pl.BlockSpec((2, 2, block_rows, depth), lambda b, where: (0, 0, b, 0))] * count,
            scratch_shapes=[pltpu.VMEM((block_rows * (colors * 2 * inner + 8), LANES), jnp.float32)],
        ),
        out_shape=[jax.ShapeDtypeStruct((2, 2, rows, depth), view.dtype)] * count,
        compiler_params=pltpu.CompilerParams(vmem_limit_bytes=PACK_VMEM),
        cost_estimate=FREE,
    )(where, *[view] * count)


def pack_vectors(view, where):
    times, rows, colors, _, inner, _ = view.shape
    depth = colors * inner // 2 * LANES

    def kernel(where, src, dst, wide):
        split_lines(src, dst, wide, 0)

    return pl.pallas_call(
        kernel,
        grid_spec=pltpu.PrefetchScalarGridSpec(
            num_scalar_prefetch=1,
            grid=(times // 2,),
            in_specs=[
                pl.BlockSpec(
                    (1, rows, colors, 1, inner, LANES), lambda t, where: (2 * t + where[0], 0, 0, 0, 0, 0)
                )
            ],
            out_specs=pl.BlockSpec((1, 2, rows, depth), lambda t, where: (t, 0, 0, 0)),
            scratch_shapes=[pltpu.VMEM((rows * colors * inner, LANES), jnp.float32)],
        ),
        out_shape=jax.ShapeDtypeStruct((times // 2, 2, rows, depth), view.dtype),
        compiler_params=pltpu.CompilerParams(vmem_limit_bytes=PACK_VMEM),
        cost_estimate=FREE,
    )(where, view)


def product(near, far, sols, where, partial, shares):
    times, _, rows, depth = near.shape
    count = len(sols)
    cols = sols[0].shape[2]
    held = [] if partial is None else [partial]

    def kernel(where, near, far, *refs):
        out = refs[-1]

        def one(sol):
            g = jnp.zeros((2 * rows, 2 * cols), jnp.float32)
            for h, vec in enumerate((near, far)):
                g += lax.dot_general(
                    vec[0].reshape(2 * rows, depth),
                    sol[h].reshape(2 * cols, depth),
                    (((1,), (1,)), ((), ())),
                    preferred_element_type=jnp.float32,
                )
            crossed = pltpu.roll(g[rows:], cols, 1)
            lane = lax.broadcasted_iota(jnp.int32, crossed.shape, 1)
            out[...] = (g[:rows] + jnp.where(lane < cols, crossed, -crossed)).reshape(out.shape)

        for n in range(count):
            pl.when(pl.program_id(0) == n)(lambda n=n: one(refs[n]))

    vec_spec = pl.BlockSpec((1, 2, rows, depth), lambda i, where: (where[i], 0, 0, 0))
    sol_spec = pl.BlockSpec(sols[0].shape, lambda i, where: (0, 0, 0, 0))
    return pl.pallas_call(
        kernel,
        grid_spec=pltpu.PrefetchScalarGridSpec(
            num_scalar_prefetch=1,
            grid=(count,),
            in_specs=[vec_spec, vec_spec] + [sol_spec] * count + [pl.BlockSpec(memory_space=pl.ANY)] * len(held),
            out_specs=pl.BlockSpec(
                (shares, 1, rows // shares, 2 * cols), lambda i, where: (0, where[i], 0, 0)
            ),
        ),
        out_shape=jax.ShapeDtypeStruct((shares, times, rows // shares, 2 * cols), jnp.float32),
        input_output_aliases={3 + count: 0} if held else {},
        compiler_params=pltpu.CompilerParams(vmem_limit_bytes=VMEM),
        cost_estimate=FREE,
    )(where, near, far, *sols, *held)


def body(solutions, eigvecs):
    shares = lax.axis_size("space")
    chips = shares // 2
    me = lax.axis_index("space")
    core = me % 2
    x, y = me // 2 // RING, me // 2 % RING

    def route(dx, dy, dc):
        return [
            (i, (((i // 2 // RING) ^ dx) * RING + (i // 2 + dy) % RING) * 2 + (i % 2 ^ dc))
            for i in range(shares)
        ]

    def chip_at(dx, dy):
        return (x ^ dx) * RING + (y + dy) % RING

    def after(where, done):
        return lax.optimization_barrier((jnp.stack(where), done))[0]

    view = tile_view(solutions, shares)
    vectors = tile_view(eigvecs, 1)
    sends = {}

    def pack(moves, done):
        chunks = pack_solutions(view, after([chip_at(*m) for m in moves] + [core], done))
        sends.update(zip(moves, chunks))
        return chunks[-1]

    def send(moves):
        return {m: lax.ppermute(sends[m], "space", route(*m, 0)) for m in moves}

    done = core
    for moves in (MOVES[:1], MOVES[1:2], MOVES[2:4], MOVES[4:] + [(0, 0)]):
        done = pack(moves, done)
    arrived = send(MOVES)
    arrived[0, 0] = sends[0, 0]
    swapped = lax.ppermute(eigvecs, "space", route(0, 0, 1))
    where = after([core], done)
    near = pack_vectors(vectors, where)
    far = pack_vectors(tile_view(swapped, 1), where)
    partial = None
    for moves in ([(0, 0)], MOVES[:1], MOVES[1:2], MOVES[2:3], MOVES[3:4], MOVES[4:]):
        where = jnp.stack([chip_at(dx, -dy) for dx, dy in moves])
        partial = product(near, far, [arrived[m] for m in moves], where, partial, shares)
    partial = lax.all_to_all(partial, "space", split_axis=0, concat_axis=0, tiled=True)
    partial = partial.reshape(chips, 2, chips, -1, partial.shape[-1])
    total = jnp.sum(partial, axis=0)
    return jnp.swapaxes(total, 0, 1).reshape(shares, -1, total.shape[-1])


def solution(mesh):
    placed = (P(("tm", "space"), None, None, None, None), P("tm", None, None, None, "space"))
    return jax.shard_map(
        body, mesh=mesh, in_specs=placed, out_specs=P("tm", "space", None), check_vma=False
    )
```

```python
import jax
import jax.numpy as jnp
from jax import lax
from jax.experimental import pallas as pl
from jax.experimental.pallas import tpu as pltpu
from jax.sharding import PartitionSpec as P

LANES = 128
VMEM = 8 * 2**20
FREE = pl.CostEstimate(flops=0, bytes_accessed=0, transcendentals=0)
RING = 4
MOVES = [(1, 2), (0, 2), (1, 0), (1, 1), (1, 3), (0, 3), (0, 1)]


def tile_view(a, groups):
    outer, rows, parts, colors, sites = a.shape
    a = a.reshape(outer, rows, parts, colors, groups, sites // groups // LANES, LANES)
    a = a.transpose(0, 1, 3, 4, 5, 2, 6)
    return pltpu.with_memory_space_constraint(a.reshape(outer, rows, colors, groups, -1, LANES), pltpu.HBM)


def split_lines(src, dst, wide, flip):
    _, rows, colors, groups, inner, _ = src.shape
    lines = colors * groups * inner
    stride = wide.shape[0] // rows
    for i in range(rows):
        wide[i * stride : i * stride + lines] = src[0, i].astype(jnp.float32).reshape(lines, LANES)
    for g in range(groups):
        for c in range(colors):
            for k in range(inner):
                picked = wide[pl.ds((c * groups + g) * inner + k, rows, stride=stride), :]
                lane = (c * (inner // 2) + k // 2) * LANES
                dst[g ^ flip, k % 2, :, pl.ds(lane, LANES)] = picked.astype(jnp.bfloat16)


def pack_solutions(view, where, block_rows=32):
    _, rows, colors, groups, inner, _ = view.shape
    count = where.shape[0] - 1
    depth = colors * inner // 2 * LANES

    def kernel(where, *refs):
        for n in range(count):
            split_lines(refs[n], refs[count + n], refs[2 * count], where[count])

    def source(n):
        return pl.BlockSpec(
            (1, block_rows, colors, 2, inner, LANES), lambda b, where: (0, b, 0, where[n], 0, 0)
        )

    return pl.pallas_call(
        kernel,
        grid_spec=pltpu.PrefetchScalarGridSpec(
            num_scalar_prefetch=1,
            grid=(rows // block_rows,),
            in_specs=[source(n) for n in range(count)],
            out_specs=[pl.BlockSpec((2, 2, block_rows, depth), lambda b, where: (0, 0, b, 0))] * count,
            scratch_shapes=[pltpu.VMEM((block_rows * (colors * 2 * inner + 8), LANES), jnp.float32)],
        ),
        out_shape=[jax.ShapeDtypeStruct((2, 2, rows, depth), view.dtype)] * count,
        compiler_params=pltpu.CompilerParams(vmem_limit_bytes=VMEM),
        cost_estimate=FREE,
    )(where, *[view] * count)


def pack_vectors(view, where):
    times, rows, colors, _, inner, _ = view.shape
    depth = colors * inner // 2 * LANES

    def kernel(where, src, dst, wide):
        split_lines(src, dst, wide, 0)

    return pl.pallas_call(
        kernel,
        grid_spec=pltpu.PrefetchScalarGridSpec(
            num_scalar_prefetch=1,
            grid=(times // 2,),
            in_specs=[
                pl.BlockSpec(
                    (1, rows, colors, 1, inner, LANES), lambda t, where: (2 * t + where[0], 0, 0, 0, 0, 0)
                )
            ],
            out_specs=pl.BlockSpec((1, 2, rows, depth), lambda t, where: (t, 0, 0, 0)),
            scratch_shapes=[pltpu.VMEM((rows * colors * inner, LANES), jnp.float32)],
        ),
        out_shape=jax.ShapeDtypeStruct((times // 2, 2, rows, depth), view.dtype),
        compiler_params=pltpu.CompilerParams(vmem_limit_bytes=VMEM),
        cost_estimate=FREE,
    )(where, view)


def product(near, far, sols, where, partial, shares):
    times, _, rows, depth = near.shape
    count = len(sols)
    cols = sols[0].shape[2]
    held = [] if partial is None else [partial]

    def kernel(where, near, far, *refs):
        out = refs[-1]

        def one(sol):
            g = jnp.zeros((2 * rows, 2 * cols), jnp.float32)
            for h, vec in enumerate((near, far)):
                g += lax.dot_general(
                    vec[0].reshape(2 * rows, depth),
                    sol[h].reshape(2 * cols, depth),
                    (((1,), (1,)), ((), ())),
                    preferred_element_type=jnp.float32,
                )
            crossed = pltpu.roll(g[rows:], cols, 1)
            lane = lax.broadcasted_iota(jnp.int32, crossed.shape, 1)
            out[...] = (g[:rows] + jnp.where(lane < cols, crossed, -crossed)).reshape(out.shape)

        for n in range(count):
            pl.when(pl.program_id(0) == n)(lambda n=n: one(refs[n]))

    vec_spec = pl.BlockSpec((1, 2, rows, depth), lambda i, where: (where[i], 0, 0, 0))
    sol_spec = pl.BlockSpec(sols[0].shape, lambda i, where: (0, 0, 0, 0))
    return pl.pallas_call(
        kernel,
        grid_spec=pltpu.PrefetchScalarGridSpec(
            num_scalar_prefetch=1,
            grid=(count,),
            in_specs=[vec_spec, vec_spec] + [sol_spec] * count + [pl.BlockSpec(memory_space=pl.ANY)] * len(held),
            out_specs=pl.BlockSpec(
                (shares, 1, rows // shares, 2 * cols), lambda i, where: (0, where[i], 0, 0)
            ),
        ),
        out_shape=jax.ShapeDtypeStruct((shares, times, rows // shares, 2 * cols), jnp.float32),
        input_output_aliases={3 + count: 0} if held else {},
        compiler_params=pltpu.CompilerParams(vmem_limit_bytes=VMEM),
        cost_estimate=FREE,
    )(where, near, far, *sols, *held)


def body(solutions, eigvecs):
    shares = lax.axis_size("space")
    chips = shares // 2
    me = lax.axis_index("space")
    core = me % 2
    x, y = me // 2 // RING, me // 2 % RING

    def route(dx, dy, dc):
        return [
            (i, (((i // 2 // RING) ^ dx) * RING + (i // 2 + dy) % RING) * 2 + (i % 2 ^ dc))
            for i in range(shares)
        ]

    def chip_at(dx, dy):
        return (x ^ dx) * RING + (y + dy) % RING

    def after(where, done):
        return lax.optimization_barrier((jnp.stack(where), done))[0]

    view = tile_view(solutions, shares)
    vectors = tile_view(eigvecs, 1)
    sends = {}

    def pack(moves, done):
        chunks = pack_solutions(view, after([chip_at(*m) for m in moves] + [core], done))
        sends.update(zip(moves, chunks))
        return chunks[-1]

    def send(moves):
        return {m: lax.ppermute(sends[m], "space", route(*m, 0)) for m in moves}

    done = core
    for moves in (MOVES[:1], MOVES[1:3], MOVES[3:5], MOVES[5:] + [(0, 0)]):
        done = pack(moves, done)
    raw = lax.optimization_barrier((eigvecs, sends[MOVES[0]]))[0]
    swapped = lax.ppermute(raw, "space", route(0, 0, 1))
    sends[MOVES[4]], swapped = lax.optimization_barrier((sends[MOVES[4]], swapped))
    arrived = send(MOVES)
    arrived[0, 0] = sends[0, 0]
    where = after([core], done)
    near = pack_vectors(vectors, where)
    far = pack_vectors(tile_view(swapped, 1), where)
    partial = None
    for moves in ([(0, 0)], MOVES[:1], MOVES[1:2], MOVES[2:3], MOVES[3:4], MOVES[4:]):
        where = jnp.stack([chip_at(dx, -dy) for dx, dy in moves])
        partial = product(near, far, [arrived[m] for m in moves], where, partial, shares)
    partial = lax.all_to_all(partial, "space", split_axis=0, concat_axis=0, tiled=True)
    partial = partial.reshape(chips, 2, chips, -1, partial.shape[-1])
    total = jnp.sum(partial, axis=0)
    return jnp.swapaxes(total, 0, 1).reshape(shares, -1, total.shape[-1])


def solution(mesh):
    placed = (P(("tm", "space"), None, None, None, None), P("tm", None, None, None, "space"))
    return jax.shard_map(
        body, mesh=mesh, in_specs=placed, out_specs=P("tm", "space", None), check_vma=False
    )
```

```python
import jax
import jax.numpy as jnp
from jax import lax
from jax.experimental import pallas as pl
from jax.experimental.pallas import tpu as pltpu
from jax.sharding import PartitionSpec as P

LANES = 128
VMEM = 8 * 2**20
FREE = pl.CostEstimate(flops=0, bytes_accessed=0, transcendentals=0)
RING = 4
MOVES = [(1, 2), (0, 2), (1, 0), (1, 1), (1, 3), (0, 3), (0, 1)]
LAST = [(0, 3), (1, 3), (0, 1)]


def tile_view(a, groups):
    outer, rows, parts, colors, sites = a.shape
    a = a.reshape(outer, rows, parts, colors, groups, sites // groups // LANES, LANES)
    a = a.transpose(0, 1, 3, 4, 5, 2, 6)
    return a.reshape(outer, rows, colors, groups, -1, LANES)


def split_lines(src, dst, wide, flip):
    _, rows, colors, groups, inner, _ = src.shape
    lines = colors * groups * inner
    stride = wide.shape[0] // rows
    for i in range(rows):
        wide[i * stride : i * stride + lines] = src[0, i].astype(jnp.float32).reshape(lines, LANES)
    for g in range(groups):
        for c in range(colors):
            for k in range(inner):
                picked = wide[pl.ds((c * groups + g) * inner + k, rows, stride=stride), :]
                lane = (c * (inner // 2) + k // 2) * LANES
                dst[g ^ flip, k % 2, :, pl.ds(lane, LANES)] = picked.astype(jnp.bfloat16)


def here():
    me = lax.axis_index("space")
    return me // (2 * RING), me // 2 % RING, me % 2


def chip_at(dx, dy):
    x, y, _ = here()
    return (x ^ dx) * RING + (y + dy) % RING


def pack_solutions(view, moves, block_rows=32):
    _, rows, colors, groups, inner, _ = view.shape
    count = len(moves)
    depth = colors * inner // 2 * LANES

    def kernel(*refs):
        for n in range(count):
            split_lines(refs[n], refs[count + n], refs[2 * count], here()[2])

    def source(move):
        return pl.BlockSpec(
            (1, block_rows, colors, 2, inner, LANES), lambda b: (0, b, 0, chip_at(*move), 0, 0)
        )

    return pl.pallas_call(
        kernel,
        grid=(rows // block_rows,),
        in_specs=[source(m) for m in moves],
        out_specs=[pl.BlockSpec((2, 2, block_rows, depth), lambda b: (0, 0, b, 0))] * count,
        scratch_shapes=[pltpu.VMEM((block_rows * (colors * 2 * inner + 8), LANES), jnp.float32)],
        out_shape=[jax.ShapeDtypeStruct((2, 2, rows, depth), view.dtype)] * count,
        compiler_params=pltpu.CompilerParams(vmem_limit_bytes=VMEM),
        cost_estimate=FREE,
    )(*[view] * count)


def pack_vectors(view):
    times, rows, colors, _, inner, _ = view.shape
    depth = colors * inner // 2 * LANES

    def kernel(src, dst, wide):
        split_lines(src, dst, wide, 0)

    return pl.pallas_call(
        kernel,
        grid=(times // 2,),
        in_specs=[
            pl.BlockSpec((1, rows, colors, 1, inner, LANES), lambda t: (2 * t + here()[2], 0, 0, 0, 0, 0))
        ],
        out_specs=pl.BlockSpec((1, 2, rows, depth), lambda t: (t, 0, 0, 0)),
        scratch_shapes=[pltpu.VMEM((rows * colors * inner, LANES), jnp.float32)],
        out_shape=jax.ShapeDtypeStruct((times // 2, 2, rows, depth), view.dtype),
        compiler_params=pltpu.CompilerParams(vmem_limit_bytes=VMEM),
        cost_estimate=FREE,
    )(view)


def product(near, far, sol, move, partial, shares):
    times, _, rows, depth = near.shape
    cols = sol.shape[2]
    held = [] if partial is None else [partial]

    def time():
        return chip_at(move[0], -move[1])

    def kernel(near, far, sol, *refs):
        out = refs[-1]
        g = jnp.zeros((2 * rows, 2 * cols), jnp.float32)
        for h, vec in enumerate((near, far)):
            g += lax.dot_general(
                vec[0].reshape(2 * rows, depth),
                sol[h].reshape(2 * cols, depth),
                (((1,), (1,)), ((), ())),
                preferred_element_type=jnp.float32,
            )
        crossed = pltpu.roll(g[rows:], cols, 1)
        lane = lax.broadcasted_iota(jnp.int32, crossed.shape, 1)
        out[...] = (g[:rows] + jnp.where(lane < cols, crossed, -crossed)).reshape(out.shape)

    vec_spec = pl.BlockSpec((1, 2, rows, depth), lambda i: (time(), 0, 0, 0))
    return pl.pallas_call(
        kernel,
        grid=(1,),
        in_specs=[vec_spec, vec_spec, pl.BlockSpec(sol.shape, lambda i: (0, 0, 0, 0))]
        + [pl.BlockSpec(memory_space=pl.ANY)] * len(held),
        out_specs=pl.BlockSpec((shares, 1, rows // shares, 2 * cols), lambda i: (0, time(), 0, 0)),
        out_shape=jax.ShapeDtypeStruct((shares, times, rows // shares, 2 * cols), jnp.float32),
        input_output_aliases={3: 0} if held else {},
        compiler_params=pltpu.CompilerParams(vmem_limit_bytes=VMEM),
        cost_estimate=FREE,
    )(near, far, sol, *held)


def body(solutions, eigvecs):
    shares = lax.axis_size("space")
    chips = shares // 2
    def route(dx, dy, dc):
        return [
            (i, (((i // 2 // RING) ^ dx) * RING + (i // 2 + dy) % RING) * 2 + (i % 2 ^ dc))
            for i in range(shares)
        ]

    def held_view(a, groups, done):
        a = lax.optimization_barrier((a, done))[0] if done is not None else a
        return pltpu.with_memory_space_constraint(tile_view(a, groups), pltpu.HBM)

    sends = {}
    done = None
    for moves in (MOVES[:1], MOVES[1:3], MOVES[3:5], MOVES[5:] + [(0, 0)]):
        chunks = pack_solutions(held_view(solutions, shares, done), moves)
        sends.update(zip(moves, chunks))
        done = chunks[-1]
    raw = lax.optimization_barrier((eigvecs, sends[MOVES[0]]))[0]
    swapped = lax.ppermute(raw, "space", route(0, 0, 1))
    sends[MOVES[4]], swapped = lax.optimization_barrier((sends[MOVES[4]], swapped))
    arrived = {m: lax.ppermute(sends[m], "space", route(*m, 0)) for m in MOVES}
    arrived[0, 0] = sends[0, 0]
    near = pack_vectors(held_view(eigvecs, 1, done))
    far = pack_vectors(tile_view(swapped, 1))
    partial = None
    for move in [(0, 0)] + MOVES[:4] + LAST:
        partial = product(near, far, arrived[move], move, partial, shares)
    partial = lax.all_to_all(partial, "space", split_axis=0, concat_axis=0, tiled=True)
    partial = partial.reshape(chips, 2, chips, -1, partial.shape[-1])
    total = jnp.sum(partial, axis=0)
    return jnp.swapaxes(total, 0, 1).reshape(shares, -1, total.shape[-1])


def solution(mesh):
    placed = (P(("tm", "space"), None, None, None, None), P("tm", None, None, None, "space"))
    return jax.shard_map(
        body, mesh=mesh, in_specs=placed, out_specs=P("tm", "space", None), check_vma=False
    )
```

```python
import jax
import jax.numpy as jnp
from jax import lax
from jax.experimental import pallas as pl
from jax.experimental.pallas import tpu as pltpu
from jax.sharding import PartitionSpec as P

LANES = 128
VMEM = 8 * 2**20
FREE = pl.CostEstimate(flops=0, bytes_accessed=0, transcendentals=0)
RING = 4
MOVES = [(1, 2), (0, 2), (1, 0), (1, 1), (0, 3), (1, 3), (0, 1)]


def tile_view(a, groups):
    outer, rows, parts, colors, sites = a.shape
    a = a.reshape(outer, rows, parts, colors, groups, sites // groups // LANES, LANES)
    a = a.transpose(0, 1, 3, 4, 5, 2, 6)
    return a.reshape(outer, rows, colors, groups, -1, LANES)


def split_lines(src, dst, wide, flip):
    _, rows, colors, groups, inner, _ = src.shape
    lines = colors * groups * inner
    stride = wide.shape[0] // rows
    for i in range(rows):
        wide[i * stride : i * stride + lines] = src[0, i].astype(jnp.float32).reshape(lines, LANES)
    for g in range(groups):
        for c in range(colors):
            for k in range(inner):
                picked = wide[pl.ds((c * groups + g) * inner + k, rows, stride=stride), :]
                lane = (c * (inner // 2) + k // 2) * LANES
                dst[g ^ flip, k % 2, :, pl.ds(lane, LANES)] = picked.astype(jnp.bfloat16)


def here():
    me = lax.axis_index("space")
    return me // (2 * RING), me // 2 % RING, me % 2


def chip_at(dx, dy):
    x, y, _ = here()
    return (x ^ dx) * RING + (y + dy) % RING


def pack_solutions(view, moves, block_rows=32):
    _, rows, colors, groups, inner, _ = view.shape
    count = len(moves)
    depth = colors * inner // 2 * LANES

    def kernel(*refs):
        for n in range(count):
            split_lines(refs[n], refs[count + n], refs[2 * count], here()[2])

    def source(move):
        return pl.BlockSpec(
            (1, block_rows, colors, 2, inner, LANES), lambda b: (0, b, 0, chip_at(*move), 0, 0)
        )

    return pl.pallas_call(
        kernel,
        grid=(rows // block_rows,),
        in_specs=[source(m) for m in moves],
        out_specs=[pl.BlockSpec((2, 2, block_rows, depth), lambda b: (0, 0, b, 0))] * count,
        scratch_shapes=[pltpu.VMEM((block_rows * (colors * 2 * inner + 8), LANES), jnp.float32)],
        out_shape=[jax.ShapeDtypeStruct((2, 2, rows, depth), view.dtype)] * count,
        compiler_params=pltpu.CompilerParams(vmem_limit_bytes=VMEM),
        cost_estimate=FREE,
    )(*[view] * count)


def pack_vectors(view):
    times, rows, colors, _, inner, _ = view.shape
    depth = colors * inner // 2 * LANES

    def kernel(src, dst, wide):
        split_lines(src, dst, wide, 0)

    return pl.pallas_call(
        kernel,
        grid=(times // 2,),
        in_specs=[
            pl.BlockSpec((1, rows, colors, 1, inner, LANES), lambda t: (2 * t + here()[2], 0, 0, 0, 0, 0))
        ],
        out_specs=pl.BlockSpec((1, 2, rows, depth), lambda t: (t, 0, 0, 0)),
        scratch_shapes=[pltpu.VMEM((rows * colors * inner, LANES), jnp.float32)],
        out_shape=jax.ShapeDtypeStruct((times // 2, 2, rows, depth), view.dtype),
        compiler_params=pltpu.CompilerParams(vmem_limit_bytes=VMEM),
        cost_estimate=FREE,
    )(view)


def product(near, far, sol, move, partial, shares):
    times, _, rows, depth = near.shape
    cols = sol.shape[2]
    held = [] if partial is None else [partial]

    def time():
        return chip_at(move[0], -move[1])

    def kernel(near, far, sol, *refs):
        out = refs[-1]
        g = jnp.zeros((2 * rows, 2 * cols), jnp.float32)
        for h, vec in enumerate((near, far)):
            g += lax.dot_general(
                vec[0].reshape(2 * rows, depth),
                sol[h].reshape(2 * cols, depth),
                (((1,), (1,)), ((), ())),
                preferred_element_type=jnp.float32,
            )
        crossed = pltpu.roll(g[rows:], cols, 1)
        lane = lax.broadcasted_iota(jnp.int32, crossed.shape, 1)
        out[...] = (g[:rows] + jnp.where(lane < cols, crossed, -crossed)).reshape(out.shape)

    vec_spec = pl.BlockSpec((1, 2, rows, depth), lambda i: (time(), 0, 0, 0))
    return pl.pallas_call(
        kernel,
        grid=(1,),
        in_specs=[vec_spec, vec_spec, pl.BlockSpec(sol.shape, lambda i: (0, 0, 0, 0))]
        + [pl.BlockSpec(memory_space=pl.ANY)] * len(held),
        out_specs=pl.BlockSpec((shares, 1, rows // shares, 2 * cols), lambda i: (0, time(), 0, 0)),
        out_shape=jax.ShapeDtypeStruct((shares, times, rows // shares, 2 * cols), jnp.float32),
        input_output_aliases={3: 0} if held else {},
        compiler_params=pltpu.CompilerParams(vmem_limit_bytes=VMEM),
        cost_estimate=FREE,
    )(near, far, sol, *held)


def add_up(partial):
    chips, cores, times, rows, cols = partial.shape

    def kernel(src, dst):
        for c in range(cores):
            total = src[0, c]
            for n in range(1, chips):
                total += src[n, c]
            dst[:, c] = total

    return pl.pallas_call(
        kernel,
        out_shape=jax.ShapeDtypeStruct((times, cores, rows, cols), partial.dtype),
        compiler_params=pltpu.CompilerParams(vmem_limit_bytes=VMEM),
        cost_estimate=FREE,
    )(partial)


def body(solutions, eigvecs):
    shares = lax.axis_size("space")
    chips = shares // 2
    def route(dx, dy, dc):
        return [
            (i, (((i // 2 // RING) ^ dx) * RING + (i // 2 + dy) % RING) * 2 + (i % 2 ^ dc))
            for i in range(shares)
        ]

    def held_view(a, groups, done):
        a = lax.optimization_barrier((a, done))[0] if done is not None else a
        return pltpu.with_memory_space_constraint(tile_view(a, groups), pltpu.HBM)

    sends = {}
    done = None
    for moves in (MOVES[:1], MOVES[1:3], MOVES[3:5], MOVES[5:] + [(0, 0)]):
        chunks = pack_solutions(held_view(solutions, shares, done), moves)
        sends.update(zip(moves, chunks))
        done = chunks[-1]
    raw = lax.optimization_barrier((eigvecs, sends[MOVES[0]]))[0]
    swapped = lax.ppermute(raw, "space", route(0, 0, 1))
    sends[MOVES[4]], swapped = lax.optimization_barrier((sends[MOVES[4]], swapped))
    arrived = {m: lax.ppermute(sends[m], "space", route(*m, 0)) for m in MOVES}
    arrived[0, 0] = sends[0, 0]
    near = pack_vectors(held_view(eigvecs, 1, done))
    far = pack_vectors(tile_view(swapped, 1))
    partial = None
    for move in [(0, 0)] + MOVES:
        partial = product(near, far, arrived[move], move, partial, shares)
    partial = lax.all_to_all(partial, "space", split_axis=0, concat_axis=0, tiled=True)
    partial = partial.reshape(chips, 2, chips, -1, partial.shape[-1])
    return add_up(partial).reshape(shares, -1, partial.shape[-1])


def solution(mesh):
    placed = (P(("tm", "space"), None, None, None, None), P("tm", None, None, None, "space"))
    return jax.shard_map(
        body, mesh=mesh, in_specs=placed, out_specs=P("tm", "space", None), check_vma=False
    )
```
